32 devices in a mesh: parts: 2 (over y), branch: 4 (over z), sub: 4 (over x, core).
Axes of the slice: x: 2, y: 2, z: 4, core: 2. Of those that a mesh axis runs over, the one named last changes fastest.
Arguments:
- charges: bfloat16 [2048, 64, 128], P(('parts', 'branch', 'sub')), parts along dimension 0, may hold values from -6 to 6
- leaf_basis: bfloat16 [2048, 64, 64], P(('parts', 'branch', 'sub')), parts along dimension 0, may hold values from -0.75 to 0.75
- leaf_transfer: bfloat16 [2048, 64, 64], P(('parts', 'branch', 'sub')), parts along dimension 0, may hold values from -0.375 to 0.375
- parent_transfer: bfloat16 [512, 64, 64], P(('parts', 'branch', 'sub')), parts along dimension 0, may hold values from -0.375 to 0.375
- near_source: int32 [2048, 8], P(('parts', 'branch', 'sub')), parts along dimension 0, may hold values from 0 to 1023, as said below
- near_block: bfloat16 [2048, 8, 64, 64], P(('parts', 'branch', 'sub')), parts along dimension 0, may hold values from -0.25 to 0.25
- local_source: int32 [2048, 4], P(('parts', 'branch', 'sub')), parts along dimension 0, may hold values from 0 to 1023, as said below
- local_count: int32 [2048], P(('parts', 'branch', 'sub')), parts along dimension 0, may hold values from 1 to 4, as said below
- local_coupling: bfloat16 [2048, 4, 64, 64], P(('parts', 'branch', 'sub')), parts along dimension 0, may hold values from -0.375 to 0.375
- remote_target: int32 [32, 32], P(('parts', 'branch', 'sub')), parts along dimension 0, may hold values from 0 to 64, as said below
- remote_source: int32 [32, 32], P(('parts', 'branch', 'sub')), parts along dimension 0, may hold values from 0 to 63
- remote_coupling: bfloat16 [32, 32, 64, 64], P(('parts', 'branch', 'sub')), parts along dimension 0, may hold values from -0.375 to 0.375
- top_source: int32 [128, 8], P(('parts', 'branch')), parts along dimension 0, may hold values from 0 to 63
- top_coupling: bfloat16 [128, 8, 64, 64], P(('parts', 'branch')), parts along dimension 0, may hold values from -0.25 to 0.25
Outputs:
- potential: bfloat16 [2048, 64, 128], P(('parts', 'branch', 'sub')), parts along dimension 0
The draws below stay inside these ranges and needn't reach their ends.
There are 2 independent parts, one for each index of `parts`. The reference program is written for one: setup_inputs(seed, part) draws one part's arguments, and reference() takes and returns one part's arrays. A program takes and returns all parts, laid end to end along the dimension named above; each array names one. Nothing has to cross between parts.
Inputs may be any that keep to these rules, and one draw needn't show every extreme that they name: `near_source`: global leaf index of a near partner of leaf b, within 4 leaves of b; in every draw some leaf has partners exactly 4 away on both sides. `local_source`: global index of a partner leaf in the same aligned block of 64 leaves as leaf b. Leaf b uses its first local_count[b] local partners; some leaf uses all 4. `remote_target`: row g is a sending device; slot s goes to device s // 2; the value is the target leaf within that device's 64 leaves, or 64 for an empty slot. In every draw some device receives 2 filled slots from every sender, and some slot is empty. `remote_source`: source leaf within the sending device's 64 leaves. `top_source`: global index of a top box coupled to top box t.
All inputs are finite; a program needn't handle non-finite values.
Results may differ from the reference program's by a relative error of at most 0.0051.
Values may be sent and summed in bfloat16 or wider, within the bound.
A program may use at most 128 MiB of HBM per device.

```python
import jax
import jax.numpy as jnp
from jax import lax

LEAF_PTS = 64
RANK = 64
VECTORS = 128
BOX_DEV = 64
NEAR = 8
LOCAL_PAIRS = 4
TOP_PAIRS = 8
CAPACITY = 2
HALO_LEAVES = 4
GROUP_DEVS = 16
LEAVES = 1024
PARENTS = 256
TOP_BRANCH = 16
TOPS = 64
SLOTS = 32
N_BRANCH = 4
N_SUB = 4


def draw_near_source(key, part):
    key = jax.random.fold_in(key, 11)
    offset_key, pick_key = jax.random.split(key)
    leaf_rows = jnp.arange(LEAVES, dtype=jnp.int32)[:, None]
    columns = jnp.arange(NEAR, dtype=jnp.int32)[None, :]
    offsets = jax.random.randint(offset_key, (LEAVES, NEAR), -HALO_LEAVES, HALO_LEAVES + 1)
    chosen = jax.random.randint(pick_key, (), HALO_LEAVES, LEAVES - HALO_LEAVES)
    offsets = jnp.where((leaf_rows == chosen) & (columns == 0), HALO_LEAVES, offsets)
    offsets = jnp.where((leaf_rows == chosen) & (columns == 1), -HALO_LEAVES, offsets)
    return jnp.clip(leaf_rows + offsets, 0, LEAVES - 1).astype(jnp.int32)


def draw_local_source(key, part):
    key = jax.random.fold_in(key, 23)
    leaf_rows = jnp.arange(LEAVES, dtype=jnp.int32)[:, None]
    within = jax.random.randint(key, (LEAVES, LOCAL_PAIRS), 0, BOX_DEV)
    return (leaf_rows // BOX_DEV * BOX_DEV + within).astype(jnp.int32)


def draw_local_count(key, part):
    key = jax.random.fold_in(key, 37)
    count_key, pick_key = jax.random.split(key)
    counts = jax.random.randint(count_key, (LEAVES,), 1, LOCAL_PAIRS + 1)
    chosen = jax.random.randint(pick_key, (), 0, LEAVES)
    return jnp.where(jnp.arange(LEAVES, dtype=jnp.int32) == chosen, LOCAL_PAIRS, counts).astype(jnp.int32)


def draw_remote_target(key, part):
    key = jax.random.fold_in(key, 53)
    fill_key, value_key, pick_key, row_key = jax.random.split(key, 4)
    owners = (jnp.arange(SLOTS, dtype=jnp.int32) // CAPACITY)[None, :]
    busiest = jax.random.randint(pick_key, (), 0, GROUP_DEVS)
    filled = (jax.random.randint(fill_key, (GROUP_DEVS, SLOTS), 0, 2) == 1) | (owners == busiest)
    values = jax.random.randint(value_key, (GROUP_DEVS, SLOTS), 0, BOX_DEV)
    sender = jax.random.randint(row_key, (), 0, GROUP_DEVS)
    senders = jnp.arange(GROUP_DEVS, dtype=jnp.int32)[:, None]
    emptied = (senders == sender) & (owners == (busiest + 1) % GROUP_DEVS)
    filled = filled & jnp.logical_not(emptied)
    return jnp.where(filled, values, BOX_DEV).astype(jnp.int32)


def with_ends(values, key, low, top_value):
    dims = values.shape
    spot = [jax.random.randint(jax.random.fold_in(key, axis), (), 0, dims[axis]) for axis in range(len(dims))]
    values = values.at[tuple(spot)].set(low)
    longest = dims.index(max(dims))
    spot[longest] = (spot[longest] + 1) % dims[longest]
    return values.at[tuple(spot)].set(top_value)


def shard_levels(stream_key, extent, cuts, low, high):
    gain = 1.0
    for position, shards_of in cuts:
        draws = jax.random.uniform(jax.random.fold_in(jax.random.fold_in(stream_key, 6), position), (shards_of,), jnp.float32, low / len(cuts), high / len(cuts))
        gain = gain * jnp.repeat(jnp.exp(draws), extent[position] // shards_of).reshape((-1,) + (1,) * (len(extent) - 1 - position))
    return gain


def scatter_about(own_key, dims, width, limit, shards=(), held_as=jnp.bfloat16):
    factor_of = shard_levels(own_key, dims, shards, -0.22, 0.18) if shards else 1.0
    entries = jax.random.normal(own_key, dims, jnp.float32) * width * factor_of
    return jnp.minimum(jnp.maximum(entries, -limit), limit).astype(held_as)


def setup_inputs(seed: int = 0, part: int = 0) -> dict:
    seeds = jax.random.split(jax.random.key(seed), 15)
    part_keys = jax.random.split(jax.random.fold_in(seeds[14], part), 15)
    return {
        "charges": scatter_about(part_keys[0], (LEAVES, LEAF_PTS, VECTORS), 1.0, 6.0, ((0, 16),)),
        "leaf_basis": scatter_about(part_keys[1], (LEAVES, LEAF_PTS, RANK), LEAF_PTS ** -0.5, 0.75, ((0, 16),)),
        "leaf_transfer": scatter_about(part_keys[2], (LEAVES, RANK, RANK), (4 * RANK) ** -0.5, 0.375, ((0, 16),)),
        "parent_transfer": scatter_about(part_keys[3], (PARENTS, RANK, RANK), (4 * RANK) ** -0.5, 0.375, ((0, 16),)),
        "near_source": draw_near_source(jax.random.fold_in(jax.random.fold_in(seeds[14], part), 71), part),
        "near_block": scatter_about(part_keys[5], (LEAVES, NEAR, LEAF_PTS, LEAF_PTS), (NEAR * LEAF_PTS) ** -0.5, 0.25, ((0, 16),)),
        "local_source": draw_local_source(jax.random.fold_in(jax.random.fold_in(seeds[14], part), 71), part),
        "local_count": draw_local_count(jax.random.fold_in(jax.random.fold_in(seeds[14], part), 71), part),
        "local_coupling": scatter_about(part_keys[8], (LEAVES, LOCAL_PAIRS, RANK, RANK), (LOCAL_PAIRS * RANK) ** -0.5, 0.375, ((0, 16),)),
        "remote_target": draw_remote_target(jax.random.fold_in(jax.random.fold_in(seeds[14], part), 71), part),
        "remote_source": with_ends(jax.random.randint(part_keys[10], (GROUP_DEVS, SLOTS), 0, BOX_DEV), jax.random.fold_in(part_keys[10], 1), 0, BOX_DEV - 1).astype(jnp.int32),
        "remote_coupling": scatter_about(part_keys[11], (GROUP_DEVS, SLOTS, RANK, RANK), (4 * RANK) ** -0.5, 0.375, ((0, 16),)),
        "top_source": with_ends(jax.random.randint(part_keys[12], (TOPS, TOP_PAIRS), 0, TOPS), jax.random.fold_in(part_keys[12], 1), 0, TOPS - 1).astype(jnp.int32),
        "top_coupling": scatter_about(part_keys[13], (TOPS, TOP_PAIRS, RANK, RANK), (TOP_PAIRS * RANK) ** -0.5, 0.25, ((0, 4),)),
    }


highest = lax.Precision.HIGHEST


def reference(charges, leaf_basis, leaf_transfer, parent_transfer, near_source, near_block, local_source, local_count, local_coupling, remote_target, remote_source, remote_coupling, top_source, top_coupling):
    leaf_coeffs = jnp.einsum('blr,blv->brv', leaf_basis.astype(jnp.float32), charges.astype(jnp.float32), precision=highest).astype(jnp.bfloat16)
    lift_mats = leaf_transfer.astype(jnp.float32).reshape(PARENTS, 4, RANK, RANK)
    children = leaf_coeffs.astype(jnp.float32).reshape(PARENTS, 4, RANK, VECTORS)
    parent_coeffs = jnp.einsum('pcrq,pcrv->pqv', lift_mats, children, precision=highest)
    raises = parent_transfer.astype(jnp.float32)
    lifted = jnp.einsum('prq,prv->pqv', raises, parent_coeffs, precision=highest)
    top_coeffs = jnp.sum(lifted.reshape(N_BRANCH, N_SUB, TOP_BRANCH, RANK, VECTORS), axis=1).reshape(TOPS, RANK, VECTORS).astype(jnp.bfloat16)
    picked = top_coeffs[top_source].astype(jnp.float32)
    top_field = jnp.einsum('tkrq,tkqv->trv', top_coupling.astype(jnp.float32), picked, precision=highest).astype(jnp.bfloat16)
    above_field = jnp.broadcast_to(top_field.astype(jnp.float32).reshape(N_BRANCH, 1, TOP_BRANCH, RANK, VECTORS), (N_BRANCH, N_SUB, TOP_BRANCH, RANK, VECTORS)).reshape(PARENTS, RANK, VECTORS)
    parent_field = jnp.einsum('prq,pqv->prv', raises, above_field, precision=highest)
    lowered = jnp.einsum('pcrq,pqv->pcrv', lift_mats, parent_field, precision=highest).reshape(LEAVES, RANK, VECTORS)

    positions = jnp.arange(LOCAL_PAIRS, dtype=jnp.int32)

    def local_block(pieces):
        sources, counts, blocks = pieces
        gathered = leaf_coeffs[sources].astype(jnp.float32)
        weights = (positions[None, :] < counts[:, None]).astype(jnp.float32)
        return jnp.einsum('bkrq,bkqv,bk->brv', blocks.astype(jnp.float32), gathered, weights, precision=highest)

    local_field = lax.map(local_block, (local_source.reshape(GROUP_DEVS, BOX_DEV, LOCAL_PAIRS), local_count.reshape(GROUP_DEVS, BOX_DEV), local_coupling.reshape(GROUP_DEVS, BOX_DEV, LOCAL_PAIRS, RANK, RANK))).reshape(LEAVES, RANK, VECTORS)

    slot_owner = jnp.arange(SLOTS, dtype=jnp.int32) // CAPACITY

    def remote_step(running, device):
        gathered = leaf_coeffs[remote_source[device] + device * BOX_DEV].astype(jnp.float32)
        outgoing = jnp.einsum('srq,sqv->srv', remote_coupling[device].astype(jnp.float32), gathered, precision=highest).astype(jnp.bfloat16)
        slot_target = remote_target[device]
        destination = jnp.where(slot_target < BOX_DEV, slot_owner * BOX_DEV + slot_target, LEAVES).astype(jnp.int32)
        return running.at[destination].add(outgoing.astype(jnp.float32), mode="drop"), None

    remote_field, unused = lax.scan(remote_step, jnp.zeros((LEAVES, RANK, VECTORS), jnp.float32), jnp.arange(GROUP_DEVS, dtype=jnp.int32))

    def near_part(pieces):
        sources, blocks = pieces
        gathered = charges[sources].astype(jnp.float32)
        return jnp.einsum('bkij,bkjv->biv', blocks.astype(jnp.float32), gathered, precision=highest)

    near_field = lax.map(near_part, (near_source.reshape(GROUP_DEVS, BOX_DEV, NEAR), near_block.reshape(GROUP_DEVS, BOX_DEV, NEAR, LEAF_PTS, LEAF_PTS))).reshape(LEAVES, LEAF_PTS, VECTORS)
    leaf_field = (lowered + local_field + remote_field).astype(jnp.bfloat16)
    far_field = jnp.einsum('blr,brv->blv', leaf_basis.astype(jnp.float32), leaf_field.astype(jnp.float32), precision=highest)
    return (far_field + near_field).astype(jnp.bfloat16)
```

```python
import functools

import jax
import jax.numpy as jnp
from jax import lax
from jax.experimental import pallas as pl
from jax.experimental.pallas import tpu as pltpu
from jax.sharding import PartitionSpec as P

HALO_LEAVES = 4
CAPACITY = 2
MESH = pl.DeviceIdType.MESH
F32 = jnp.float32
BF16 = jnp.bfloat16


def side_by_side(mats, values):
    return jnp.dot(
        jnp.concatenate(mats, axis=1),
        jnp.concatenate(values, axis=0),
        preferred_element_type=F32,
    )


def across(mat, value):
    return lax.dot_general(mat, value, (((0,), (0,)), ((), ())), preferred_element_type=F32)


def loop(start, stop, unroll, compute, store):
    assert (stop - start) % unroll == 0

    def body(step, carry):
        first = start + step * unroll
        results = [compute(first + i) for i in range(unroll)]
        for i, result in enumerate(results):
            store(first + i, result)
        return carry

    lax.fori_loop(0, (stop - start) // unroll, body, 0)


def kernel(
    branch_size,
    sub_size,
    near_src,
    local_src,
    local_cnt,
    remote_src,
    top_src,
    remote_tgt,
    charges_hbm,
    basis_hbm,
    transfer_hbm,
    raise_hbm,
    near_hbm,
    local_hbm,
    remote_hbm,
    top_hbm,
    out_hbm,
    padded,
    basis,
    transfer,
    raises,
    near,
    local,
    remote,
    top,
    coeffs,
    near_field,
    local_field,
    outgoing,
    arrived,
    chain,
    parent,
    lifted,
    partial,
    partials,
    tops,
    field,
    leaf_field,
    result,
    label_tile,
    labels,
    prev_vec,
    last_vec,
    prev_idx,
    last_idx,
    load_sem,
    out_sem,
    idx_sem,
    halo_send,
    halo_recv,
    label_send,
    label_recv,
    slot_send,
    slot_recv,
    part_send,
    part_recv,
    up_send,
    up_recv,
    far_send,
    far_recv,
    twin_send,
    twin_recv,
):
    parts = lax.axis_index("parts")
    branch = lax.axis_index("branch")
    sub = lax.axis_index("sub")
    devices = branch_size * sub_size
    me = branch * sub_size + sub
    boxes = basis.shape[0]
    rank, vectors = coeffs.shape[1:]
    assert sub_size == 4 and boxes & (boxes - 1) == 0
    slots = devices * CAPACITY
    parents = boxes // 4
    owned = parents // sub_size
    near_count, local_room, top_pairs = near.shape[1], local.shape[1], top.shape[1]
    before = me * boxes - HALO_LEAVES

    def at(peer):
        return (parts, lax.div(peer, sub_size), lax.rem(peer, sub_size))

    def peer_of(i):
        return lax.rem(me + i, devices)

    loads = [
        (charges_hbm, padded.at[pl.ds(HALO_LEAVES, boxes)]),
        (basis_hbm, basis),
        (transfer_hbm, transfer),
        (raise_hbm, raises),
        (remote_hbm.at[0], remote),
        (local_hbm, local),
        (near_hbm, near),
        (top_hbm, top),
    ]
    loads = [pltpu.make_async_copy(a, b, load_sem.at[i]) for i, (a, b) in enumerate(loads)]
    for load in loads:
        load.start()

    barrier = pltpu.get_barrier_semaphore()

    def greet(i, carry):
        pl.semaphore_signal(barrier, inc=1, device_id=at(peer_of(i)), device_id_type=MESH)
        return carry

    lax.fori_loop(1, devices, greet, 0)
    label_tile[...] = jnp.broadcast_to(remote_tgt[...], label_tile.shape)
    pl.semaphore_wait(barrier, devices - 1)

    halo_up = pltpu.make_async_remote_copy(
        src_ref=charges_hbm.at[pl.ds(boxes - HALO_LEAVES, HALO_LEAVES)],
        dst_ref=padded.at[pl.ds(0, HALO_LEAVES)],
        send_sem=halo_send.at[0],
        recv_sem=halo_recv.at[0],
        device_id=at(peer_of(1)),
        device_id_type=MESH,
    )
    halo_down = pltpu.make_async_remote_copy(
        src_ref=charges_hbm.at[pl.ds(0, HALO_LEAVES)],
        dst_ref=padded.at[pl.ds(HALO_LEAVES + boxes, HALO_LEAVES)],
        send_sem=halo_send.at[1],
        recv_sem=halo_recv.at[1],
        device_id=at(peer_of(devices - 1)),
        device_id_type=MESH,
    )
    halo_up.start()
    halo_down.start()

    def label_copy(peer, slot):
        return pltpu.make_async_remote_copy(
            src_ref=label_tile,
            dst_ref=labels.at[slot],
            send_sem=label_send.at[peer],
            recv_sem=label_recv.at[slot],
            device_id=at(peer),
            device_id_type=MESH,
        )

    def send_label(i, carry):
        label_copy(peer_of(i), me).start()
        return carry

    lax.fori_loop(1, devices, send_label, 0)
    labels[me] = label_tile[...]

    loads[0].wait()
    loads[1].wait()

    def put_coeffs(b, value):
        coeffs[b] = value.astype(BF16)

    loop(0, boxes, 8, lambda b: across(basis[b], padded[HALO_LEAVES + b]), put_coeffs)
    coeffs[boxes] = jnp.zeros((rank, vectors), BF16)
    loads[2].wait()
    loads[3].wait()

    def put_parent(p, value):
        parent[p] = value.astype(BF16)

    def lift(p):
        four = pl.ds(pl.multiple_of(p * 4, 4), 4)
        return across(
            transfer[four].reshape(4 * rank, rank), coeffs[four].reshape(4 * rank, vectors)
        )

    loop(0, parents, 4, lift, put_parent)

    def put_lifted(p, value):
        lifted[p] = value
        partial[p] = value.astype(BF16)

    loop(0, parents, 4, lambda p: across(raises[p], parent[p]), put_lifted)

    def part_copy(other, slot):
        return pltpu.make_async_remote_copy(
            src_ref=partial.at[pl.ds(other * owned, owned)],
            dst_ref=partials.at[slot],
            send_sem=part_send.at[other],
            recv_sem=part_recv.at[slot],
            device_id=(parts, branch, other),
            device_id_type=MESH,
        )

    for i in range(1, sub_size):
        part_copy(lax.rem(sub + i, sub_size), sub).start()

    loads[4].wait()

    def contribution(s):
        return jnp.dot(remote[s], coeffs[remote_src[0, s]], preferred_element_type=F32)

    def put_outgoing(s, value):
        outgoing[lax.div(s, CAPACITY), lax.rem(s, CAPACITY)] = value.astype(BF16)

    loop(0, slots, 8, contribution, put_outgoing)

    def slot_copy(peer, slot):
        return pltpu.make_async_remote_copy(
            src_ref=outgoing.at[peer],
            dst_ref=arrived.at[slot],
            send_sem=slot_send.at[peer],
            recv_sem=slot_recv.at[slot],
            device_id=at(peer),
            device_id_type=MESH,
        )

    def send_slots(i, carry):
        slot_copy(peer_of(i), me).start()
        return carry

    lax.fori_loop(1, devices, send_slots, 0)
    arrived[me] = outgoing[me]

    def local_product(b):
        used = local_cnt[b]
        chosen = [
            coeffs[jnp.where(k < used, local_src[b, k] & (boxes - 1), boxes)]
            for k in range(local_room)
        ]
        return side_by_side([local[b, k] for k in range(local_room)], chosen)

    def put_local(b, value):
        local_field[b] = value

    def near_product(b):
        chosen = [
            padded[jnp.clip(near_src[b, k] - before, 0, boxes + 2 * HALO_LEAVES - 1)]
            for k in range(near_count)
        ]
        return side_by_side([near[b, k] for k in range(near_count)], chosen)

    def put_near(b, value):
        near_field[b] = value

    quarter = boxes // 4
    loads[5].wait()
    loop(0, boxes // 2, 2, local_product, put_local)

    for i in range(1, sub_size):
        part_copy(sub, lax.rem(sub + i, sub_size)).wait_recv()
    for j in range(owned):
        total = lifted[sub * owned + j]
        for i in range(1, sub_size):
            total += partials[lax.rem(sub + i, sub_size), j].astype(F32)
        tops[branch, sub, j] = total.astype(BF16)

    far_sub = sub + sub_size // 2 - (sub // (sub_size // 2)) * sub_size
    twin_sub = sub + 1 - 2 * lax.rem(sub, 2)
    twin_far = far_sub + 1 - 2 * lax.rem(far_sub, 2)

    def top_copy(owner_branch, owner_sub, send_sem, recv_sem, target):
        block = tops.at[owner_branch, owner_sub]
        return pltpu.make_async_remote_copy(
            src_ref=block,
            dst_ref=block,
            send_sem=send_sem,
            recv_sem=recv_sem,
            device_id=target,
            device_id_type=MESH,
        )

    def up_copy(other, owner):
        return top_copy(owner, sub, up_send.at[other], up_recv.at[owner], (parts, other, sub))

    def far_copy(owner, column):
        return top_copy(
            owner, column, far_send.at[owner], far_recv.at[owner], (parts, branch, far_sub)
        )

    def twin_copy(owner, column, which):
        return top_copy(
            owner,
            column,
            twin_send.at[which, owner],
            twin_recv.at[which, owner],
            (parts, branch, twin_sub),
        )

    def other_branch(i):
        return lax.rem(branch + i, branch_size)

    def send_up(i, carry):
        up_copy(other_branch(i), branch).start()
        return carry

    def pass_on(i, carry):
        owner = other_branch(i)
        up_copy(branch, owner).wait_recv()
        far_copy(owner, sub).start()
        twin_copy(owner, sub, 0).start()
        return carry

    def pass_twin(i, carry):
        owner = other_branch(i)
        far_copy(owner, far_sub).wait_recv()
        twin_copy(owner, far_sub, 1).start()
        return carry

    def take_twin(i, carry):
        twin_copy(i, twin_sub, 0).wait_recv()
        twin_copy(i, twin_far, 1).wait_recv()
        return carry

    lax.fori_loop(1, branch_size, send_up, 0)
    far_copy(branch, sub).start()
    twin_copy(branch, sub, 0).start()

    loop(boxes // 2, boxes, 2, local_product, put_local)
    loads[6].wait()
    halo_up.wait_recv()
    halo_down.wait_recv()
    loop(0, quarter, 2, near_product, put_near)
    lax.fori_loop(1, branch_size, pass_on, 0)
    loop(quarter, 2 * quarter, 2, near_product, put_near)
    lax.fori_loop(0, branch_size, pass_twin, 0)
    loop(2 * quarter, boxes, 2, near_product, put_near)

    def take_label(i, carry):
        label_copy(me, peer_of(i)).wait_recv()
        return carry

    lax.fori_loop(1, devices, take_label, 0)
    rows = jnp.max(labels[...], axis=1)
    lane = lax.broadcasted_iota(jnp.int32, rows.shape, 1)
    columns = [
        jnp.max(jnp.where(lane == me * CAPACITY + c, rows, -1), axis=1, keepdims=True)
        for c in range(CAPACITY)
    ]
    wide = prev_vec.shape[1]
    slot_lane = lax.broadcasted_iota(jnp.int32, (devices, wide), 1)
    slot_row = lax.broadcasted_iota(jnp.int32, (devices, wide), 0) * CAPACITY
    along = sum(
        jnp.sum(jnp.where(slot_lane == slot_row + c, columns[c], 0), axis=0, keepdims=True)
        for c in range(CAPACITY)
    )
    prev = jnp.full((1, wide), -1, jnp.int32)
    for c in range(CAPACITY):
        same = (columns[c] == along) & (slot_row + c < slot_lane)
        prev = jnp.maximum(
            prev, jnp.max(jnp.where(same, slot_row + c, -1), axis=0, keepdims=True)
        )
    broad = last_vec.shape[1]
    box_lane = lax.broadcasted_iota(jnp.int32, (devices, broad), 1)
    box_row = lax.broadcasted_iota(jnp.int32, (devices, broad), 0) * CAPACITY
    last = jnp.full((1, broad), -1, jnp.int32)
    for c in range(CAPACITY):
        last = jnp.maximum(
            last,
            jnp.max(jnp.where(columns[c] == box_lane, box_row + c, -1), axis=0, keepdims=True),
        )
    prev_vec[...] = jnp.broadcast_to(jnp.where(prev < 0, slots, prev), prev_vec.shape)
    last_vec[...] = jnp.broadcast_to(jnp.where(last < 0, slots, last), last_vec.shape)
    prev_copy = pltpu.make_async_copy(prev_vec, prev_idx, idx_sem.at[0])
    last_copy = pltpu.make_async_copy(last_vec, last_idx, idx_sem.at[1])
    prev_copy.start()
    last_copy.start()

    def take_slots(i, carry):
        slot_copy(me, peer_of(i)).wait_recv()
        return carry

    lax.fori_loop(1, devices, take_slots, 0)
    prev_copy.wait()
    last_copy.wait()
    chain[slots] = jnp.zeros((rank, vectors), F32)

    def link(s, carry):
        value = arrived[lax.div(s, CAPACITY), lax.rem(s, CAPACITY)].astype(F32)
        chain[s] = value + chain[prev_idx[0, s]]
        return carry

    lax.fori_loop(0, slots, link, 0)

    loads[7].wait()
    lax.fori_loop(0, branch_size, take_twin, 0)

    def top_product(t):
        chosen = []
        for k in range(top_pairs):
            source = top_src[t, k]
            owner = lax.div(source, parents)
            inner = lax.rem(source, parents)
            chosen.append(tops[owner, lax.div(inner, owned), lax.rem(inner, owned)])
        return side_by_side([top[t, k] for k in range(top_pairs)], chosen)

    def put_field(t, value):
        field[t] = value.astype(BF16)

    loop(0, parents, 4, top_product, put_field)
    loop(
        0,
        parents,
        8,
        lambda p: jnp.dot(raises[p], field[p], preferred_element_type=F32),
        put_parent,
    )

    def lower(p):
        four = pl.ds(pl.multiple_of(p * 4, 4), 4)
        return jnp.dot(
            transfer[four].reshape(4 * rank, rank), parent[p], preferred_element_type=F32
        )

    def put_leaf(p, value):
        for c in range(4):
            b = p * 4 + c
            whole = value[c * rank : (c + 1) * rank] + local_field[b] + chain[last_idx[0, b]]
            leaf_field[b] = whole.astype(BF16)

    loop(0, parents, 2, lower, put_leaf)

    def potential(b):
        return near_field[b] + jnp.dot(basis[b], leaf_field[b], preferred_element_type=F32)

    def put_result(b, value):
        result[b] = value.astype(BF16)

    stores = []
    for piece in range(4):
        loop(piece * quarter, (piece + 1) * quarter, 8, potential, put_result)
        rows_of = pl.ds(piece * quarter, quarter)
        stores.append(
            pltpu.make_async_copy(result.at[rows_of], out_hbm.at[rows_of], out_sem.at[piece])
        )
        stores[-1].start()

    halo_up.wait_send()
    halo_down.wait_send()

    def sent(i, carry):
        peer = peer_of(i)
        label_copy(peer, me).wait_send()
        slot_copy(peer, me).wait_send()
        return carry

    lax.fori_loop(1, devices, sent, 0)
    for i in range(1, sub_size):
        part_copy(lax.rem(sub + i, sub_size), sub).wait_send()

    def sent_up(i, carry):
        up_copy(other_branch(i), branch).wait_send()
        return carry

    lax.fori_loop(1, branch_size, sent_up, 0)

    def sent_on(i, carry):
        far_copy(i, sub).wait_send()
        twin_copy(i, sub, 0).wait_send()
        twin_copy(i, far_sub, 1).wait_send()
        return carry

    lax.fori_loop(0, branch_size, sent_on, 0)
    for store in stores:
        store.wait()


def on_device(
    charges,
    leaf_basis,
    leaf_transfer,
    parent_transfer,
    near_source,
    near_block,
    local_source,
    local_count,
    local_coupling,
    remote_target,
    remote_source,
    remote_coupling,
    top_source,
    top_coupling,
):
    boxes, points, vectors = charges.shape
    rank = leaf_basis.shape[2]
    branch_size, sub_size = lax.axis_size("branch"), lax.axis_size("sub")
    devices = branch_size * sub_size
    slots = remote_target.shape[1]
    parents = parent_transfer.shape[0]
    owned = parents // sub_size
    wide = -(-slots // 128) * 128
    broad = -(-boxes // 128) * 128
    vmem = pltpu.VMEM
    dma = pltpu.SemaphoreType.DMA
    scratch = [
        vmem((boxes + 2 * HALO_LEAVES, points, vectors), BF16),
        vmem(leaf_basis.shape, BF16),
        vmem(leaf_transfer.shape, BF16),
        vmem(parent_transfer.shape, BF16),
        vmem(near_block.shape, BF16),
        vmem(local_coupling.shape, BF16),
        vmem(remote_coupling.shape[1:], BF16),
        vmem(top_coupling.shape, BF16),
        vmem((boxes + 1, rank, vectors), BF16),
        vmem((boxes, points, vectors), F32),
        vmem((boxes, rank, vectors), F32),
        vmem((devices, CAPACITY, rank, vectors), BF16),
        vmem((devices, CAPACITY, rank, vectors), BF16),
        vmem((slots + 1, rank, vectors), F32),
        vmem((parents, rank, vectors), BF16),
        vmem((parents, rank, vectors), F32),
        vmem((parents, rank, vectors), BF16),
        vmem((sub_size, owned, rank, vectors), BF16),
        vmem((branch_size, sub_size, owned, rank, vectors), BF16),
        vmem((parents, rank, vectors), BF16),
        vmem((boxes, rank, vectors), BF16),
        vmem((boxes, points, vectors), BF16),
        vmem((8, slots), jnp.int32),
        vmem((devices, 8, slots), jnp.int32),
        vmem((8, wide), jnp.int32),
        vmem((8, broad), jnp.int32),
        pltpu.SMEM((8, wide), jnp.int32),
        pltpu.SMEM((8, broad), jnp.int32),
        dma((8,)),
        dma((4,)),
        dma((2,)),
        dma((2,)),
        dma((2,)),
        dma((devices,)),
        dma((devices,)),
        dma((devices,)),
        dma((devices,)),
        dma((sub_size,)),
        dma((sub_size,)),
        dma((branch_size,)),
        dma((branch_size,)),
        dma((branch_size,)),
        dma((branch_size,)),
        dma((2, branch_size)),
        dma((2, branch_size)),
    ]
    smem = pl.BlockSpec(memory_space=pltpu.SMEM)
    anywhere = pl.BlockSpec(memory_space=pl.ANY)
    return pl.pallas_call(
        functools.partial(kernel, branch_size, sub_size),
        out_shape=jax.ShapeDtypeStruct((boxes, points, vectors), BF16),
        in_specs=[smem] * 5 + [pl.BlockSpec(memory_space=pltpu.VMEM)] + [anywhere] * 8,
        out_specs=anywhere,
        scratch_shapes=scratch,
        compiler_params=pltpu.CompilerParams(
            collective_id=0, has_side_effects=True, vmem_limit_bytes=60 * 2**20
        ),
    )(
        near_source,
        local_source,
        local_count,
        remote_source,
        top_source,
        remote_target,
        charges,
        leaf_basis,
        leaf_transfer,
        parent_transfer,
        near_block,
        local_coupling,
        remote_coupling,
        top_coupling,
    )


def solution(mesh):
    boxed = P(("parts", "branch", "sub"))
    topped = P(("parts", "branch"))
    return jax.shard_map(
        on_device,
        mesh=mesh,
        in_specs=(boxed,) * 12 + (topped, topped),
        out_specs=boxed,
        check_vma=False,
    )
```

```python
import functools

import jax
import jax.numpy as jnp
from jax import lax
from jax.experimental import pallas as pl
from jax.experimental.pallas import tpu as pltpu
from jax.sharding import PartitionSpec as P

HALO_LEAVES = 4
CAPACITY = 2
MESH = pl.DeviceIdType.MESH
EARLY = 5
NU, LU, TU = 8, 16, 8
F32 = jnp.float32
BF16 = jnp.bfloat16


def side_by_side(mats, values):
    return jnp.dot(
        jnp.concatenate(mats, axis=1),
        jnp.concatenate(values, axis=0),
        preferred_element_type=F32,
    )


def across(mat, value):
    return lax.dot_general(mat, value, (((0,), (0,)), ((), ())), preferred_element_type=F32)


def loop(start, stop, unroll, compute, store):
    assert (stop - start) % unroll == 0

    def body(step, carry):
        first = start + step * unroll
        results = [compute(first + i) for i in range(unroll)]
        for i, result in enumerate(results):
            store(first + i, result)
        return carry

    lax.fori_loop(0, (stop - start) // unroll, body, 0)


def kernel(
    branch_size,
    sub_size,
    near_src_hbm,
    local_src_hbm,
    local_cnt_hbm,
    remote_src_hbm,
    top_src_hbm,
    remote_tgt_hbm,
    charges_hbm,
    basis_hbm,
    transfer_hbm,
    raise_hbm,
    near_hbm,
    local_hbm,
    remote_hbm,
    top_hbm,
    out_hbm,
    near_src,
    local_src,
    local_cnt,
    remote_src,
    top_src,
    remote_tgt,
    padded,
    basis,
    transfer,
    raises,
    near,
    local,
    remote,
    top,
    coeffs,
    near_field,
    local_field,
    outgoing,
    arrived,
    chain,
    parent,
    lifted,
    partial,
    partials,
    tops,
    field,
    leaf_field,
    result,
    label_tile,
    labels,
    prev_vec,
    last_vec,
    prev_idx,
    last_idx,
    load_sem,
    out_sem,
    idx_sem,
    halo_send,
    halo_recv,
    label_send,
    label_recv,
    slot_send,
    slot_recv,
    part_send,
    part_recv,
    up_send,
    up_recv,
    far_send,
    far_recv,
    twin_send,
    twin_recv,
):
    parts = lax.axis_index("parts")
    branch = lax.axis_index("branch")
    sub = lax.axis_index("sub")
    devices = branch_size * sub_size
    me = branch * sub_size + sub
    boxes = basis.shape[0]
    rank, vectors = coeffs.shape[1:]
    assert sub_size == 4 and boxes & (boxes - 1) == 0
    slots = devices * CAPACITY
    early = 1 + (devices - 1) * EARLY // 15
    parents = boxes // 4
    owned = parents // sub_size
    near_count, local_room, top_pairs = near.shape[1], local.shape[1], top.shape[1]
    before = me * boxes - HALO_LEAVES

    def at(peer):
        return (parts, lax.div(peer, sub_size), lax.rem(peer, sub_size))

    def peer_of(i):
        return lax.rem(me + i, devices)

    loads = [
        (charges_hbm, padded.at[pl.ds(HALO_LEAVES, boxes)]),
        (basis_hbm, basis),
        (transfer_hbm, transfer),
        (raise_hbm, raises),
        (remote_hbm.at[0], remote),
        (local_hbm, local),
        (near_hbm, near),
        (top_hbm, top),
        (remote_tgt_hbm, remote_tgt),
        (remote_src_hbm, remote_src),
        (local_src_hbm, local_src),
        (local_cnt_hbm, local_cnt),
        (near_src_hbm, near_src),
        (top_src_hbm, top_src),
    ]
    loads = [pltpu.make_async_copy(a, b, load_sem.at[i]) for i, (a, b) in enumerate(loads)]
    for load in loads[8:] + loads[:5]:
        load.start()

    barrier = pltpu.get_barrier_semaphore()

    def greet(i, carry):
        pl.semaphore_signal(barrier, inc=1, device_id=at(peer_of(i)), device_id_type=MESH)
        return carry

    lax.fori_loop(1, devices, greet, 0)
    loads[8].wait()
    label_tile[...] = jnp.broadcast_to(remote_tgt[...], label_tile.shape)
    pl.semaphore_wait(barrier, devices - 1)

    halo_up = pltpu.make_async_remote_copy(
        src_ref=charges_hbm.at[pl.ds(boxes - HALO_LEAVES, HALO_LEAVES)],
        dst_ref=padded.at[pl.ds(0, HALO_LEAVES)],
        send_sem=halo_send.at[0],
        recv_sem=halo_recv.at[0],
        device_id=at(peer_of(1)),
        device_id_type=MESH,
    )
    halo_down = pltpu.make_async_remote_copy(
        src_ref=charges_hbm.at[pl.ds(0, HALO_LEAVES)],
        dst_ref=padded.at[pl.ds(HALO_LEAVES + boxes, HALO_LEAVES)],
        send_sem=halo_send.at[1],
        recv_sem=halo_recv.at[1],
        device_id=at(peer_of(devices - 1)),
        device_id_type=MESH,
    )
    halo_up.start()
    halo_down.start()

    def label_copy(peer, slot):
        return pltpu.make_async_remote_copy(
            src_ref=label_tile,
            dst_ref=labels.at[slot],
            send_sem=label_send.at[peer],
            recv_sem=label_recv.at[slot],
            device_id=at(peer),
            device_id_type=MESH,
        )

    def send_label(i, carry):
        label_copy(peer_of(i), me).start()
        return carry

    lax.fori_loop(1, devices, send_label, 0)
    labels[me] = label_tile[...]

    loads[0].wait()
    loads[1].wait()
    for load in loads[5:8]:
        load.start()

    def put_coeffs(b, value):
        coeffs[b] = value.astype(BF16)

    loop(0, boxes, 8, lambda b: across(basis[b], padded[HALO_LEAVES + b]), put_coeffs)
    coeffs[boxes] = jnp.zeros((rank, vectors), BF16)
    loads[2].wait()
    loads[3].wait()

    def put_parent(p, value):
        parent[p] = value.astype(BF16)

    def lift(p):
        four = pl.ds(pl.multiple_of(p * 4, 4), 4)
        return across(
            transfer[four].reshape(4 * rank, rank), coeffs[four].reshape(4 * rank, vectors)
        )

    loop(0, parents, 4, lift, put_parent)

    def put_lifted(p, value):
        lifted[p] = value
        partial[p] = value.astype(BF16)

    loop(0, parents, 4, lambda p: across(raises[p], parent[p]), put_lifted)

    def part_copy(other, slot):
        return pltpu.make_async_remote_copy(
            src_ref=partial.at[pl.ds(other * owned, owned)],
            dst_ref=partials.at[slot],
            send_sem=part_send.at[other],
            recv_sem=part_recv.at[slot],
            device_id=(parts, branch, other),
            device_id_type=MESH,
        )

    for i in range(1, sub_size):
        part_copy(lax.rem(sub + i, sub_size), sub).start()

    loads[4].wait()
    loads[9].wait()

    def contribution(s):
        return jnp.dot(remote[s], coeffs[remote_src[0, s]], preferred_element_type=F32)

    def put_outgoing(s, value):
        outgoing[lax.div(s, CAPACITY), lax.rem(s, CAPACITY)] = value.astype(BF16)

    loop(0, slots, 8, contribution, put_outgoing)

    def slot_copy(peer, slot):
        return pltpu.make_async_remote_copy(
            src_ref=outgoing.at[peer],
            dst_ref=arrived.at[slot],
            send_sem=slot_send.at[peer],
            recv_sem=slot_recv.at[slot],
            device_id=at(peer),
            device_id_type=MESH,
        )

    def send_slots(i, carry):
        slot_copy(peer_of(i), me).start()
        return carry

    lax.fori_loop(1, early, send_slots, 0)
    arrived[me] = outgoing[me]

    def local_product(b):
        used = local_cnt[b]
        chosen = [
            coeffs[jnp.where(k < used, local_src[k, b] & (boxes - 1), boxes)]
            for k in range(local_room)
        ]
        return side_by_side([local[b, k] for k in range(local_room)], chosen)

    def put_local(b, value):
        local_field[b] = value

    def near_product(b):
        chosen = [
            padded[jnp.clip(near_src[k, b] - before, 0, boxes + 2 * HALO_LEAVES - 1)]
            for k in range(near_count)
        ]
        return side_by_side([near[b, k] for k in range(near_count)], chosen)

    def put_near(b, value):
        near_field[b] = value

    quarter = boxes // 4
    loads[5].wait()
    loads[10].wait()
    loads[11].wait()
    loop(0, boxes // 2, LU, local_product, put_local)

    for i in range(1, sub_size):
        part_copy(sub, lax.rem(sub + i, sub_size)).wait_recv()
    for j in range(owned):
        total = lifted[sub * owned + j]
        for i in range(1, sub_size):
            total += partials[lax.rem(sub + i, sub_size), j].astype(F32)
        tops[branch, sub, j] = total.astype(BF16)

    far_sub = sub + sub_size // 2 - (sub // (sub_size // 2)) * sub_size
    twin_sub = sub + 1 - 2 * lax.rem(sub, 2)
    twin_far = far_sub + 1 - 2 * lax.rem(far_sub, 2)

    def top_copy(owner_branch, owner_sub, send_sem, recv_sem, target):
        block = tops.at[owner_branch, owner_sub]
        return pltpu.make_async_remote_copy(
            src_ref=block,
            dst_ref=block,
            send_sem=send_sem,
            recv_sem=recv_sem,
            device_id=target,
            device_id_type=MESH,
        )

    def up_copy(other, owner):
        return top_copy(owner, sub, up_send.at[other], up_recv.at[owner], (parts, other, sub))

    def far_copy(owner, column):
        return top_copy(
            owner, column, far_send.at[owner], far_recv.at[owner], (parts, branch, far_sub)
        )

    def twin_copy(owner, column, which):
        return top_copy(
            owner,
            column,
            twin_send.at[which, owner],
            twin_recv.at[which, owner],
            (parts, branch, twin_sub),
        )

    def other_branch(i):
        return lax.rem(branch + i, branch_size)

    def send_up(i, carry):
        up_copy(other_branch(i), branch).start()
        return carry

    def pass_on(i, carry):
        owner = other_branch(i)
        up_copy(branch, owner).wait_recv()
        far_copy(owner, sub).start()
        twin_copy(owner, sub, 0).start()
        return carry

    def pass_twin(i, carry):
        owner = other_branch(i)
        far_copy(owner, far_sub).wait_recv()
        twin_copy(owner, far_sub, 1).start()
        return carry

    def take_twin(i, carry):
        twin_copy(i, twin_sub, 0).wait_recv()
        twin_copy(i, twin_far, 1).wait_recv()
        return carry

    lax.fori_loop(1, branch_size, send_up, 0)
    far_copy(branch, sub).start()
    twin_copy(branch, sub, 0).start()

    loop(boxes // 2, boxes, LU, local_product, put_local)
    loads[6].wait()
    loads[12].wait()
    halo_up.wait_recv()
    halo_down.wait_recv()
    loop(0, quarter, NU, near_product, put_near)
    lax.fori_loop(1, branch_size, pass_on, 0)
    lax.fori_loop(early, devices, send_slots, 0)
    loop(quarter, 2 * quarter, NU, near_product, put_near)
    lax.fori_loop(0, branch_size, pass_twin, 0)
    loop(2 * quarter, boxes, NU, near_product, put_near)

    def take_label(i, carry):
        label_copy(me, peer_of(i)).wait_recv()
        return carry

    lax.fori_loop(1, devices, take_label, 0)
    rows = jnp.max(labels[...], axis=1)
    lane = lax.broadcasted_iota(jnp.int32, rows.shape, 1)
    columns = [
        jnp.max(jnp.where(lane == me * CAPACITY + c, rows, -1), axis=1, keepdims=True)
        for c in range(CAPACITY)
    ]
    wide = prev_vec.shape[1]
    slot_lane = lax.broadcasted_iota(jnp.int32, (devices, wide), 1)
    slot_row = lax.broadcasted_iota(jnp.int32, (devices, wide), 0) * CAPACITY
    along = sum(
        jnp.sum(jnp.where(slot_lane == slot_row + c, columns[c], 0), axis=0, keepdims=True)
        for c in range(CAPACITY)
    )
    prev = jnp.full((1, wide), -1, jnp.int32)
    for c in range(CAPACITY):
        same = (columns[c] == along) & (slot_row + c < slot_lane)
        prev = jnp.maximum(
            prev, jnp.max(jnp.where(same, slot_row + c, -1), axis=0, keepdims=True)
        )
    broad = last_vec.shape[1]
    box_lane = lax.broadcasted_iota(jnp.int32, (devices, broad), 1)
    box_row = lax.broadcasted_iota(jnp.int32, (devices, broad), 0) * CAPACITY
    last = jnp.full((1, broad), -1, jnp.int32)
    for c in range(CAPACITY):
        last = jnp.maximum(
            last,
            jnp.max(jnp.where(columns[c] == box_lane, box_row + c, -1), axis=0, keepdims=True),
        )
    prev_vec[...] = jnp.broadcast_to(jnp.where(prev < 0, slots, prev), prev_vec.shape)
    last_vec[...] = jnp.broadcast_to(jnp.where(last < 0, slots, last), last_vec.shape)
    prev_copy = pltpu.make_async_copy(prev_vec, prev_idx, idx_sem.at[0])
    last_copy = pltpu.make_async_copy(last_vec, last_idx, idx_sem.at[1])
    prev_copy.start()
    last_copy.start()

    def take_slots(i, carry):
        slot_copy(me, peer_of(i)).wait_recv()
        return carry

    lax.fori_loop(1, devices, take_slots, 0)
    prev_copy.wait()
    last_copy.wait()
    chain[slots] = jnp.zeros((rank, vectors), F32)

    def link(s, carry):
        value = arrived[lax.div(s, CAPACITY), lax.rem(s, CAPACITY)].astype(F32)
        chain[s] = value + chain[prev_idx[0, s]]
        return carry

    lax.fori_loop(0, slots, link, 0)

    loads[7].wait()
    loads[13].wait()
    lax.fori_loop(0, branch_size, take_twin, 0)

    def top_product(t):
        chosen = []
        for k in range(top_pairs):
            source = top_src[k, t]
            owner = lax.div(source, parents)
            inner = lax.rem(source, parents)
            chosen.append(tops[owner, lax.div(inner, owned), lax.rem(inner, owned)])
        return side_by_side([top[t, k] for k in range(top_pairs)], chosen)

    def put_field(t, value):
        field[t] = value.astype(BF16)

    loop(0, parents, TU, top_product, put_field)
    loop(
        0,
        parents,
        8,
        lambda p: jnp.dot(raises[p], field[p], preferred_element_type=F32),
        put_parent,
    )

    def lower(p):
        four = pl.ds(pl.multiple_of(p * 4, 4), 4)
        return jnp.dot(
            transfer[four].reshape(4 * rank, rank), parent[p], preferred_element_type=F32
        )

    def put_leaf(p, value):
        for c in range(4):
            b = p * 4 + c
            whole = value[c * rank : (c + 1) * rank] + local_field[b] + chain[last_idx[0, b]]
            leaf_field[b] = whole.astype(BF16)

    loop(0, parents, 2, lower, put_leaf)

    def potential(b):
        return near_field[b] + jnp.dot(basis[b], leaf_field[b], preferred_element_type=F32)

    def put_result(b, value):
        result[b] = value.astype(BF16)

    stores = []
    for piece in range(4):
        loop(piece * quarter, (piece + 1) * quarter, 8, potential, put_result)
        rows_of = pl.ds(piece * quarter, quarter)
        stores.append(
            pltpu.make_async_copy(result.at[rows_of], out_hbm.at[rows_of], out_sem.at[piece])
        )
        stores[-1].start()

    halo_up.wait_send()
    halo_down.wait_send()

    def sent(i, carry):
        peer = peer_of(i)
        label_copy(peer, me).wait_send()
        slot_copy(peer, me).wait_send()
        return carry

    lax.fori_loop(1, devices, sent, 0)
    for i in range(1, sub_size):
        part_copy(lax.rem(sub + i, sub_size), sub).wait_send()

    def sent_up(i, carry):
        up_copy(other_branch(i), branch).wait_send()
        return carry

    lax.fori_loop(1, branch_size, sent_up, 0)

    def sent_on(i, carry):
        far_copy(i, sub).wait_send()
        twin_copy(i, sub, 0).wait_send()
        twin_copy(i, far_sub, 1).wait_send()
        return carry

    lax.fori_loop(0, branch_size, sent_on, 0)
    for store in stores:
        store.wait()


def on_device(
    charges,
    leaf_basis,
    leaf_transfer,
    parent_transfer,
    near_source,
    near_block,
    local_source,
    local_count,
    local_coupling,
    remote_target,
    remote_source,
    remote_coupling,
    top_source,
    top_coupling,
):
    boxes, points, vectors = charges.shape
    rank = leaf_basis.shape[2]
    branch_size, sub_size = lax.axis_size("branch"), lax.axis_size("sub")
    devices = branch_size * sub_size
    slots = remote_target.shape[1]
    parents = parent_transfer.shape[0]
    owned = parents // sub_size
    wide = -(-slots // 128) * 128
    broad = -(-boxes // 128) * 128
    vmem = pltpu.VMEM
    dma = pltpu.SemaphoreType.DMA
    smem = pltpu.SMEM
    scratch = [
        smem(near_source.shape[::-1], jnp.int32),
        smem(local_source.shape[::-1], jnp.int32),
        smem(local_count.shape, jnp.int32),
        smem(remote_source.shape, jnp.int32),
        smem(top_source.shape[::-1], jnp.int32),
        vmem(remote_target.shape, jnp.int32),
        vmem((boxes + 2 * HALO_LEAVES, points, vectors), BF16),
        vmem(leaf_basis.shape, BF16),
        vmem(leaf_transfer.shape, BF16),
        vmem(parent_transfer.shape, BF16),
        vmem(near_block.shape, BF16),
        vmem(local_coupling.shape, BF16),
        vmem(remote_coupling.shape[1:], BF16),
        vmem(top_coupling.shape, BF16),
        vmem((boxes + 1, rank, vectors), BF16),
        vmem((boxes, points, vectors), F32),
        vmem((boxes, rank, vectors), F32),
        vmem((devices, CAPACITY, rank, vectors), BF16),
        vmem((devices, CAPACITY, rank, vectors), BF16),
        vmem((slots + 1, rank, vectors), F32),
        vmem((parents, rank, vectors), BF16),
        vmem((parents, rank, vectors), F32),
        vmem((parents, rank, vectors), BF16),
        vmem((sub_size, owned, rank, vectors), BF16),
        vmem((branch_size, sub_size, owned, rank, vectors), BF16),
        vmem((parents, rank, vectors), BF16),
        vmem((boxes, rank, vectors), BF16),
        vmem((boxes, points, vectors), BF16),
        vmem((8, slots), jnp.int32),
        vmem((devices, 8, slots), jnp.int32),
        vmem((8, wide), jnp.int32),
        vmem((8, broad), jnp.int32),
        pltpu.SMEM((8, wide), jnp.int32),
        pltpu.SMEM((8, broad), jnp.int32),
        dma((14,)),
        dma((4,)),
        dma((2,)),
        dma((2,)),
        dma((2,)),
        dma((devices,)),
        dma((devices,)),
        dma((devices,)),
        dma((devices,)),
        dma((sub_size,)),
        dma((sub_size,)),
        dma((branch_size,)),
        dma((branch_size,)),
        dma((branch_size,)),
        dma((branch_size,)),
        dma((2, branch_size)),
        dma((2, branch_size)),
    ]
    anywhere = pl.BlockSpec(memory_space=pl.ANY)
    return pl.pallas_call(
        functools.partial(kernel, branch_size, sub_size),
        out_shape=jax.ShapeDtypeStruct((boxes, points, vectors), BF16),
        in_specs=[anywhere] * 14,
        out_specs=anywhere,
        scratch_shapes=scratch,
        compiler_params=pltpu.CompilerParams(
            collective_id=0, has_side_effects=True, vmem_limit_bytes=60 * 2**20
        ),
    )(
        near_source.T,
        local_source.T,
        local_count,
        remote_source,
        top_source.T,
        remote_target,
        charges,
        leaf_basis,
        leaf_transfer,
        parent_transfer,
        near_block,
        local_coupling,
        remote_coupling,
        top_coupling,
    )


def solution(mesh):
    boxed = P(("parts", "branch", "sub"))
    topped = P(("parts", "branch"))
    return jax.shard_map(
        on_device,
        mesh=mesh,
        in_specs=(boxed,) * 12 + (topped, topped),
        out_specs=boxed,
        check_vma=False,
    )
```

```python
import functools

import jax
import jax.numpy as jnp
from jax import lax
from jax.experimental import pallas as pl
from jax.experimental.pallas import tpu as pltpu
from jax.sharding import PartitionSpec as P

HALO_LEAVES = 4
CAPACITY = 2
MESH = pl.DeviceIdType.MESH
EARLY = 5
NU, LU, TU = 8, 16, 8
F32 = jnp.float32
BF16 = jnp.bfloat16


def side_by_side(mats, values):
    return jnp.dot(
        jnp.concatenate(mats, axis=1),
        jnp.concatenate(values, axis=0),
        preferred_element_type=F32,
    )


def across(mat, value):
    return lax.dot_general(mat, value, (((0,), (0,)), ((), ())), preferred_element_type=F32)


def loop(start, stop, unroll, compute, store):
    assert (stop - start) % unroll == 0

    def body(step, carry):
        first = start + step * unroll
        results = [compute(first + i) for i in range(unroll)]
        for i, result in enumerate(results):
            store(first + i, result)
        return carry

    lax.fori_loop(0, (stop - start) // unroll, body, 0)


def kernel(
    branch_size,
    sub_size,
    near_src_hbm,
    local_src_hbm,
    local_cnt_hbm,
    remote_src_hbm,
    top_src_hbm,
    remote_tgt_hbm,
    charges_hbm,
    basis_hbm,
    transfer_hbm,
    raise_hbm,
    near_hbm,
    local_hbm,
    remote_hbm,
    top_hbm,
    out_hbm,
    near_src,
    local_src,
    local_cnt,
    remote_src,
    top_src,
    remote_tgt,
    padded,
    basis,
    transfer,
    raises,
    near,
    local,
    remote,
    top,
    coeffs,
    near_field,
    local_field,
    outgoing,
    arrived,
    chain,
    parent,
    lifted,
    partial,
    partials,
    tops,
    field,
    result,
    label_tile,
    labels,
    prev_vec,
    last_vec,
    prev_idx,
    last_idx,
    load_sem,
    out_sem,
    idx_sem,
    halo_send,
    halo_recv,
    label_send,
    label_recv,
    slot_send,
    slot_recv,
    part_send,
    part_recv,
    up_send,
    up_recv,
    far_send,
    far_recv,
    twin_send,
    twin_recv,
):
    parts = lax.axis_index("parts")
    branch = lax.axis_index("branch")
    sub = lax.axis_index("sub")
    devices = branch_size * sub_size
    me = branch * sub_size + sub
    boxes = basis.shape[0]
    rank, vectors = coeffs.shape[1:]
    assert sub_size == 4 and boxes & (boxes - 1) == 0
    slots = devices * CAPACITY
    early = 1 + (devices - 1) * EARLY // 15
    parents = boxes // 4
    owned = parents // sub_size
    near_count, local_room, top_pairs = near.shape[1], local.shape[1], top.shape[1]
    before = me * boxes - HALO_LEAVES

    def at(peer):
        return (parts, lax.div(peer, sub_size), lax.rem(peer, sub_size))

    def peer_of(i):
        return lax.rem(me + i, devices)

    loads = [
        (charges_hbm, padded.at[pl.ds(HALO_LEAVES, boxes)]),
        (basis_hbm, basis),
        (transfer_hbm, transfer),
        (raise_hbm, raises),
        (remote_hbm.at[0], remote),
        (local_hbm, local),
        (near_hbm, near),
        (top_hbm, top),
        (remote_tgt_hbm, remote_tgt),
        (remote_src_hbm, remote_src),
        (local_src_hbm, local_src),
        (local_cnt_hbm, local_cnt),
        (near_src_hbm, near_src),
        (top_src_hbm, top_src),
    ]
    loads = [pltpu.make_async_copy(a, b, load_sem.at[i]) for i, (a, b) in enumerate(loads)]
    for load in loads[8:] + loads[:5]:
        load.start()

    barrier = pltpu.get_barrier_semaphore()

    def greet(i, carry):
        pl.semaphore_signal(barrier, inc=1, device_id=at(peer_of(i)), device_id_type=MESH)
        return carry

    lax.fori_loop(1, devices, greet, 0)
    loads[8].wait()
    label_tile[...] = jnp.broadcast_to(remote_tgt[...], label_tile.shape)
    pl.semaphore_wait(barrier, devices - 1)

    halo_up = pltpu.make_async_remote_copy(
        src_ref=charges_hbm.at[pl.ds(boxes - HALO_LEAVES, HALO_LEAVES)],
        dst_ref=padded.at[pl.ds(0, HALO_LEAVES)],
        send_sem=halo_send.at[0],
        recv_sem=halo_recv.at[0],
        device_id=at(peer_of(1)),
        device_id_type=MESH,
    )
    halo_down = pltpu.make_async_remote_copy(
        src_ref=charges_hbm.at[pl.ds(0, HALO_LEAVES)],
        dst_ref=padded.at[pl.ds(HALO_LEAVES + boxes, HALO_LEAVES)],
        send_sem=halo_send.at[1],
        recv_sem=halo_recv.at[1],
        device_id=at(peer_of(devices - 1)),
        device_id_type=MESH,
    )
    halo_up.start()
    halo_down.start()

    def label_copy(peer, slot):
        return pltpu.make_async_remote_copy(
            src_ref=label_tile,
            dst_ref=labels.at[slot],
            send_sem=label_send.at[peer],
            recv_sem=label_recv.at[slot],
            device_id=at(peer),
            device_id_type=MESH,
        )

    def send_label(i, carry):
        label_copy(peer_of(i), me).start()
        return carry

    lax.fori_loop(1, devices, send_label, 0)
    labels[me] = label_tile[...]

    loads[0].wait()
    loads[1].wait()
    for load in loads[5:8]:
        load.start()

    def put_coeffs(b, value):
        coeffs[b] = value.astype(BF16)

    loop(0, boxes, 8, lambda b: across(basis[b], padded[HALO_LEAVES + b]), put_coeffs)
    coeffs[boxes] = jnp.zeros((rank, vectors), BF16)
    loads[2].wait()
    loads[3].wait()

    def put_parent(p, value):
        parent[p] = value.astype(BF16)

    def lift(p):
        four = pl.ds(pl.multiple_of(p * 4, 4), 4)
        return across(
            transfer[four].reshape(4 * rank, rank), coeffs[four].reshape(4 * rank, vectors)
        )

    loop(0, parents, 4, lift, put_parent)

    def put_lifted(p, value):
        lifted[p] = value
        partial[p] = value.astype(BF16)

    loop(0, parents, 4, lambda p: across(raises[p], parent[p]), put_lifted)

    def part_copy(other, slot):
        return pltpu.make_async_remote_copy(
            src_ref=partial.at[pl.ds(other * owned, owned)],
            dst_ref=partials.at[slot],
            send_sem=part_send.at[other],
            recv_sem=part_recv.at[slot],
            device_id=(parts, branch, other),
            device_id_type=MESH,
        )

    for i in range(1, sub_size):
        part_copy(lax.rem(sub + i, sub_size), sub).start()

    loads[4].wait()
    loads[9].wait()

    def contribution(s):
        return jnp.dot(remote[s], coeffs[remote_src[0, s]], preferred_element_type=F32)

    def put_outgoing(s, value):
        outgoing[lax.div(s, CAPACITY), lax.rem(s, CAPACITY)] = value.astype(BF16)

    loop(0, slots, 8, contribution, put_outgoing)

    def slot_copy(peer, slot):
        return pltpu.make_async_remote_copy(
            src_ref=outgoing.at[peer],
            dst_ref=arrived.at[slot],
            send_sem=slot_send.at[peer],
            recv_sem=slot_recv.at[slot],
            device_id=at(peer),
            device_id_type=MESH,
        )

    def send_slots(i, carry):
        slot_copy(peer_of(i), me).start()
        return carry

    lax.fori_loop(1, early, send_slots, 0)
    arrived[me] = outgoing[me]

    def local_product(b):
        used = local_cnt[b]
        chosen = [
            coeffs[jnp.where(k < used, local_src[k, b] & (boxes - 1), boxes)]
            for k in range(local_room)
        ]
        return side_by_side([local[b, k] for k in range(local_room)], chosen)

    def put_local(b, value):
        local_field[b] = value

    def near_product(b):
        chosen = [
            padded[jnp.clip(near_src[k, b] - before, 0, boxes + 2 * HALO_LEAVES - 1)]
            for k in range(near_count)
        ]
        return side_by_side([near[b, k] for k in range(near_count)], chosen)

    def put_near(b, value):
        near_field[b] = value

    quarter = boxes // 4
    loads[5].wait()
    loads[10].wait()
    loads[11].wait()
    loop(0, boxes // 2, LU, local_product, put_local)

    for i in range(1, sub_size):
        part_copy(sub, lax.rem(sub + i, sub_size)).wait_recv()
    for j in range(owned):
        total = lifted[sub * owned + j]
        for i in range(1, sub_size):
            total += partials[lax.rem(sub + i, sub_size), j].astype(F32)
        tops[branch, sub, j] = total.astype(BF16)

    far_sub = sub + sub_size // 2 - (sub // (sub_size // 2)) * sub_size
    twin_sub = sub + 1 - 2 * lax.rem(sub, 2)
    twin_far = far_sub + 1 - 2 * lax.rem(far_sub, 2)

    def top_copy(owner_branch, owner_sub, send_sem, recv_sem, target):
        block = tops.at[owner_branch, owner_sub]
        return pltpu.make_async_remote_copy(
            src_ref=block,
            dst_ref=block,
            send_sem=send_sem,
            recv_sem=recv_sem,
            device_id=target,
            device_id_type=MESH,
        )

    def up_copy(other, owner):
        return top_copy(owner, sub, up_send.at[other], up_recv.at[owner], (parts, other, sub))

    def far_copy(owner, column):
        return top_copy(
            owner, column, far_send.at[owner], far_recv.at[owner], (parts, branch, far_sub)
        )

    def twin_copy(owner, column, which):
        return top_copy(
            owner,
            column,
            twin_send.at[which, owner],
            twin_recv.at[which, owner],
            (parts, branch, twin_sub),
        )

    def other_branch(i):
        return lax.rem(branch + i, branch_size)

    def send_up(i, carry):
        up_copy(other_branch(i), branch).start()
        return carry

    def pass_on(i, carry):
        owner = other_branch(i)
        up_copy(branch, owner).wait_recv()
        far_copy(owner, sub).start()
        twin_copy(owner, sub, 0).start()
        return carry

    def pass_twin(i, carry):
        owner = other_branch(i)
        far_copy(owner, far_sub).wait_recv()
        twin_copy(owner, far_sub, 1).start()
        return carry

    def take_twin(i, carry):
        twin_copy(i, twin_sub, 0).wait_recv()
        twin_copy(i, twin_far, 1).wait_recv()
        return carry

    lax.fori_loop(1, branch_size, send_up, 0)
    far_copy(branch, sub).start()
    twin_copy(branch, sub, 0).start()

    loop(boxes // 2, boxes, LU, local_product, put_local)
    loads[6].wait()
    loads[12].wait()
    halo_up.wait_recv()
    halo_down.wait_recv()
    loop(0, quarter, NU, near_product, put_near)
    lax.fori_loop(1, branch_size, pass_on, 0)
    lax.fori_loop(early, devices, send_slots, 0)
    loop(quarter, 2 * quarter, NU, near_product, put_near)
    lax.fori_loop(0, branch_size, pass_twin, 0)
    loop(2 * quarter, boxes, NU, near_product, put_near)

    def take_label(i, carry):
        label_copy(me, peer_of(i)).wait_recv()
        return carry

    lax.fori_loop(1, devices, take_label, 0)
    rows = jnp.max(labels[...], axis=1)
    lane = lax.broadcasted_iota(jnp.int32, rows.shape, 1)
    columns = [
        jnp.max(jnp.where(lane == me * CAPACITY + c, rows, -1), axis=1, keepdims=True)
        for c in range(CAPACITY)
    ]
    wide = prev_vec.shape[1]
    slot_lane = lax.broadcasted_iota(jnp.int32, (devices, wide), 1)
    slot_row = lax.broadcasted_iota(jnp.int32, (devices, wide), 0) * CAPACITY
    along = sum(
        jnp.sum(jnp.where(slot_lane == slot_row + c, columns[c], 0), axis=0, keepdims=True)
        for c in range(CAPACITY)
    )
    prev = jnp.full((1, wide), -1, jnp.int32)
    for c in range(CAPACITY):
        same = (columns[c] == along) & (slot_row + c < slot_lane)
        prev = jnp.maximum(
            prev, jnp.max(jnp.where(same, slot_row + c, -1), axis=0, keepdims=True)
        )
    broad = last_vec.shape[1]
    box_lane = lax.broadcasted_iota(jnp.int32, (devices, broad), 1)
    box_row = lax.broadcasted_iota(jnp.int32, (devices, broad), 0) * CAPACITY
    last = jnp.full((1, broad), -1, jnp.int32)
    for c in range(CAPACITY):
        last = jnp.maximum(
            last,
            jnp.max(jnp.where(columns[c] == box_lane, box_row + c, -1), axis=0, keepdims=True),
        )
    prev_vec[...] = jnp.broadcast_to(jnp.where(prev < 0, slots, prev), prev_vec.shape)
    last_vec[...] = jnp.broadcast_to(jnp.where(last < 0, slots, last), last_vec.shape)
    prev_copy = pltpu.make_async_copy(prev_vec, prev_idx, idx_sem.at[0])
    last_copy = pltpu.make_async_copy(last_vec, last_idx, idx_sem.at[1])
    prev_copy.start()
    last_copy.start()

    loads[7].wait()
    loads[13].wait()
    lax.fori_loop(0, branch_size, take_twin, 0)

    def top_product(t):
        chosen = []
        for k in range(top_pairs):
            source = top_src[k, t]
            owner = lax.div(source, parents)
            inner = lax.rem(source, parents)
            chosen.append(tops[owner, lax.div(inner, owned), lax.rem(inner, owned)])
        return side_by_side([top[t, k] for k in range(top_pairs)], chosen)

    def put_field(t, value):
        field[t] = value.astype(BF16)

    loop(0, parents, TU, top_product, put_field)
    loop(
        0,
        parents,
        8,
        lambda p: jnp.dot(raises[p], field[p], preferred_element_type=F32),
        put_parent,
    )

    def lower(p):
        four = pl.ds(pl.multiple_of(p * 4, 4), 4)
        return jnp.dot(
            transfer[four].reshape(4 * rank, rank), parent[p], preferred_element_type=F32
        )

    def put_leaf(p, value):
        for c in range(4):
            b = p * 4 + c
            local_field[b] += value[c * rank : (c + 1) * rank]

    loop(0, parents, 2, lower, put_leaf)

    def take_slots(i, carry):
        slot_copy(me, peer_of(i)).wait_recv()
        return carry

    lax.fori_loop(1, devices, take_slots, 0)
    prev_copy.wait()
    last_copy.wait()
    chain[slots] = jnp.zeros((rank, vectors), F32)

    def link(s, carry):
        value = arrived[lax.div(s, CAPACITY), lax.rem(s, CAPACITY)].astype(F32)
        chain[s] = value + chain[prev_idx[0, s]]
        return carry

    lax.fori_loop(0, slots, link, 0)

    def potential(b):
        leaf_field = (local_field[b] + chain[last_idx[0, b]]).astype(BF16)
        return near_field[b] + jnp.dot(basis[b], leaf_field, preferred_element_type=F32)

    def put_result(b, value):
        result[b] = value.astype(BF16)

    stores = []
    for piece in range(4):
        loop(piece * quarter, (piece + 1) * quarter, 8, potential, put_result)
        rows_of = pl.ds(piece * quarter, quarter)
        stores.append(
            pltpu.make_async_copy(result.at[rows_of], out_hbm.at[rows_of], out_sem.at[piece])
        )
        stores[-1].start()

    halo_up.wait_send()
    halo_down.wait_send()

    def sent(i, carry):
        peer = peer_of(i)
        label_copy(peer, me).wait_send()
        slot_copy(peer, me).wait_send()
        return carry

    lax.fori_loop(1, devices, sent, 0)
    for i in range(1, sub_size):
        part_copy(lax.rem(sub + i, sub_size), sub).wait_send()

    def sent_up(i, carry):
        up_copy(other_branch(i), branch).wait_send()
        return carry

    lax.fori_loop(1, branch_size, sent_up, 0)

    def sent_on(i, carry):
        far_copy(i, sub).wait_send()
        twin_copy(i, sub, 0).wait_send()
        twin_copy(i, far_sub, 1).wait_send()
        return carry

    lax.fori_loop(0, branch_size, sent_on, 0)
    for store in stores:
        store.wait()


def on_device(
    charges,
    leaf_basis,
    leaf_transfer,
    parent_transfer,
    near_source,
    near_block,
    local_source,
    local_count,
    local_coupling,
    remote_target,
    remote_source,
    remote_coupling,
    top_source,
    top_coupling,
):
    boxes, points, vectors = charges.shape
    rank = leaf_basis.shape[2]
    branch_size, sub_size = lax.axis_size("branch"), lax.axis_size("sub")
    devices = branch_size * sub_size
    slots = remote_target.shape[1]
    parents = parent_transfer.shape[0]
    owned = parents // sub_size
    wide = -(-slots // 128) * 128
    broad = -(-boxes // 128) * 128
    vmem = pltpu.VMEM
    dma = pltpu.SemaphoreType.DMA
    smem = pltpu.SMEM
    scratch = [
        smem(near_source.shape[::-1], jnp.int32),
        smem(local_source.shape[::-1], jnp.int32),
        smem(local_count.shape, jnp.int32),
        smem(remote_source.shape, jnp.int32),
        smem(top_source.shape[::-1], jnp.int32),
        vmem(remote_target.shape, jnp.int32),
        vmem((boxes + 2 * HALO_LEAVES, points, vectors), BF16),
        vmem(leaf_basis.shape, BF16),
        vmem(leaf_transfer.shape, BF16),
        vmem(parent_transfer.shape, BF16),
        vmem(near_block.shape, BF16),
        vmem(local_coupling.shape, BF16),
        vmem(remote_coupling.shape[1:], BF16),
        vmem(top_coupling.shape, BF16),
        vmem((boxes + 1, rank, vectors), BF16),
        vmem((boxes, points, vectors), F32),
        vmem((boxes, rank, vectors), F32),
        vmem((devices, CAPACITY, rank, vectors), BF16),
        vmem((devices, CAPACITY, rank, vectors), BF16),
        vmem((slots + 1, rank, vectors), F32),
        vmem((parents, rank, vectors), BF16),
        vmem((parents, rank, vectors), F32),
        vmem((parents, rank, vectors), BF16),
        vmem((sub_size, owned, rank, vectors), BF16),
        vmem((branch_size, sub_size, owned, rank, vectors), BF16),
        vmem((parents, rank, vectors), BF16),
        vmem((boxes, points, vectors), BF16),
        vmem((8, slots), jnp.int32),
        vmem((devices, 8, slots), jnp.int32),
        vmem((8, wide), jnp.int32),
        vmem((8, broad), jnp.int32),
        pltpu.SMEM((8, wide), jnp.int32),
        pltpu.SMEM((8, broad), jnp.int32),
        dma((14,)),
        dma((4,)),
        dma((2,)),
        dma((2,)),
        dma((2,)),
        dma((devices,)),
        dma((devices,)),
        dma((devices,)),
        dma((devices,)),
        dma((sub_size,)),
        dma((sub_size,)),
        dma((branch_size,)),
        dma((branch_size,)),
        dma((branch_size,)),
        dma((branch_size,)),
        dma((2, branch_size)),
        dma((2, branch_size)),
    ]
    anywhere = pl.BlockSpec(memory_space=pl.ANY)
    return pl.pallas_call(
        functools.partial(kernel, branch_size, sub_size),
        out_shape=jax.ShapeDtypeStruct((boxes, points, vectors), BF16),
        in_specs=[anywhere] * 14,
        out_specs=anywhere,
        scratch_shapes=scratch,
        compiler_params=pltpu.CompilerParams(
            collective_id=0, has_side_effects=True, vmem_limit_bytes=60 * 2**20
        ),
    )(
        near_source.T,
        local_source.T,
        local_count,
        remote_source,
        top_source.T,
        remote_target,
        charges,
        leaf_basis,
        leaf_transfer,
        parent_transfer,
        near_block,
        local_coupling,
        remote_coupling,
        top_coupling,
    )


def solution(mesh):
    boxed = P(("parts", "branch", "sub"))
    topped = P(("parts", "branch"))
    return jax.shard_map(
        on_device,
        mesh=mesh,
        in_specs=(boxed,) * 12 + (topped, topped),
        out_specs=boxed,
        check_vma=False,
    )
```
